512 devices in a mesh: frames: 64 (over z, y_hi, core), mp: 4 (over x), dp: 2 (over y_lo).
Axes of the slice: x: 4, y: 4 (y_hi: 2, y_lo: 2; y = y_hi * 2 + y_lo), z: 16, core: 2. Of those that a mesh axis runs over, the one named last changes fastest.
Arguments:
- projections: bfloat16 [2, 128, 96, 3, 3584], P('dp', 'frames', None, None, 'mp'), may hold values from -18 to 18
- perturbation: bfloat16 [2, 128, 96, 3, 3584], P('dp', 'frames', None, None, 'mp'), may hold values from -44 to 44
- out_weight: bfloat16 [3584, 3584], P('frames', 'mp'), may hold values from -0.09375 to 0.09375
- norm_gain: float32 [3584], P('mp'), may hold values from 0.25 to 1.75
- live_counts: int32 [2, 128], P('dp'), may hold values from 72 to 96, as said below
Outputs:
- features: bfloat16 [2, 128, 96, 3584], P('dp', 'frames', None, 'mp')
- penalty: float32 [2], P('dp')
- gain_grad: float32 [3584], P('mp')
The draws below stay inside these ranges and needn't reach their ends.
Inputs may be any that keep to these rules, and one draw needn't show every extreme that they name: `live_counts`: in each clip one slot has all 96 tokens live and another has 72 live.
All inputs are finite; a program needn't handle non-finite values.
Results may differ from the reference program's by a relative error of at most 0.0057.
Values may be sent and summed in bfloat16 or wider, within the bound.
A program may use at most 64 MiB of HBM per device.

```python
import math
import jax
import jax.numpy as jnp
from jax import lax

D = 3584
HEADS = 28
HEAD_DIM = 128
TILE = 96
FRAMES = 128
TOKENS = 12288
CLIPS = 2


def draw_projections(key, part):
    key = jax.random.fold_in(key, 11)
    array_shape = (CLIPS, FRAMES, TILE, 3, D)
    values = jnp.clip(jax.random.normal(key, array_shape, jnp.float32), -6.0, 6.0)
    return values.astype(jnp.bfloat16)


def draw_perturbation(key, part):
    key = jax.random.fold_in(key, 23)
    array_shape = (CLIPS, FRAMES, TILE, 3, D)
    frame_pos = jnp.arange(FRAMES).astype(jnp.float32)[None, :, None, None, None]
    rising = 1.0 + 2.0 * frame_pos / (FRAMES - 1)
    values = jnp.clip(jax.random.normal(key, array_shape, jnp.float32), -6.0, 6.0) * rising
    return values.astype(jnp.bfloat16)


def draw_live_counts(key, part):
    key = jax.random.fold_in(key, 37)
    first_key, second_key = jax.random.split(key)
    counts = jax.random.randint(first_key, (CLIPS, FRAMES), 3 * TILE // 4, TILE + 1)
    chosen = jax.random.randint(second_key, (CLIPS, 1), 0, FRAMES)
    column = jnp.arange(FRAMES)[None, :]
    counts = jnp.where(column == chosen, TILE, counts)
    counts = jnp.where(column == (chosen + FRAMES // 2) % FRAMES, 3 * TILE // 4, counts)
    return counts.astype(jnp.int32)


def level_of(own_key, extent, pieces, low, high):
    def one(dim, parts):
        heights = jax.random.uniform(jax.random.fold_in(jax.random.fold_in(own_key, 6), dim), (parts,), jnp.float32, low / len(pieces), high / len(pieces))
        return jnp.repeat(jnp.exp(heights), extent[dim] // parts).reshape((-1,) + (1,) * (len(extent) - dim - 1))

    level = one(*pieces[0])
    for cut in pieces[1:]:
        level = level * one(*cut)
    return level


def noise(own_key, extent, deviation, limit, pieces=(), dtype=jnp.bfloat16):
    entries = jax.random.normal(own_key, extent, jnp.float32) * deviation
    if len(pieces) > 0:
        entries = level_of(own_key, extent, pieces, -0.22, 0.18) * entries
    return jnp.clip(entries, min=-limit, max=limit).astype(dtype)


def setup_inputs(seed: int = 0) -> dict:
    key_of = jax.random.split(jax.random.key(seed), 6)
    projections = draw_projections(jax.random.fold_in(key_of[5], 71), 0)
    perturbation = draw_perturbation(jax.random.fold_in(key_of[5], 71), 0)
    out_weight = noise(key_of[2], (D, D), D ** -0.5, 0.09375, ((0, 64), (1, 4)))
    norm_gain = jnp.clip(1.0 + 0.15 * jax.random.normal(key_of[3], (D,), jnp.float32), 0.25, 1.75)
    live_counts = draw_live_counts(jax.random.fold_in(key_of[5], 71), 0)
    return {"projections": projections, "perturbation": perturbation, "out_weight": out_weight, "norm_gain": norm_gain, "live_counts": live_counts}


sigma_noise = 0.25
epsilon = 1e-06

def attend(query_rows, key_rows, value_rows, key_live):
    scores = jnp.einsum('rhe,mhe->hrm', query_rows.astype(jnp.float32), key_rows.astype(jnp.float32)) * (1.0 / math.sqrt(HEAD_DIM))
    masked = jnp.where(key_live[None, None, :], scores, -1e+30)
    largest = lax.optimization_barrier(jnp.max(masked, axis=-1, keepdims=True))
    weights = jnp.exp(masked - largest) * key_live[None, None, :].astype(jnp.float32)
    probabilities = (weights / lax.optimization_barrier(jnp.sum(weights, axis=-1, keepdims=True))).astype(jnp.bfloat16)
    mixed = jnp.einsum('hrm,mhe->rhe', probabilities.astype(jnp.float32), value_rows.astype(jnp.float32))
    return mixed.astype(jnp.bfloat16)

def stream_attention(stream, counts):
    padded = jnp.pad(stream, ((1, 1), (0, 0), (0, 0), (0, 0)))
    padded_counts = jnp.pad(counts, (1, 1))
    live_tokens = jnp.arange(TILE)[None, :] < padded_counts[:, None]
    windows = padded.reshape((FRAMES + 2) // 2, 2 * TILE, 3, HEADS, HEAD_DIM)
    live_windows = live_tokens.reshape((FRAMES + 2) // 2, 2 * TILE)

    def one_window(item):
        block, window_live = item
        return attend(block[:, 0], block[:, 1], block[:, 2], window_live)
    result = lax.map(one_window, (windows, live_windows))
    return result.reshape(FRAMES + 2, TILE, D)[1:-1]

def reference(projections, perturbation, out_weight, norm_gain, live_counts):
    perturbed = (projections.astype(jnp.float32) + sigma_noise * perturbation.astype(jnp.float32)).astype(jnp.bfloat16)
    live_mask = (jnp.arange(TILE)[None, None, :] < live_counts[:, :, None]).astype(jnp.float32)[..., None]
    normed_list = []
    for stream in (projections, perturbed):
        attended = jnp.stack([stream_attention(stream[clip_index], live_counts[clip_index]) for clip_index in range(CLIPS)])
        projected = jnp.dot(attended.reshape(-1, D), out_weight, preferred_element_type=jnp.float32).reshape(CLIPS, FRAMES, TILE, D)
        squares = lax.optimization_barrier(jnp.sum(projected * projected, axis=-1, keepdims=True))
        normed_list.append(projected * lax.rsqrt(squares / D + epsilon))
    normed_clean, normed_perturbed = normed_list
    features = (normed_clean * norm_gain * live_mask).astype(jnp.bfloat16)
    difference = (normed_perturbed - normed_clean) * live_mask
    feature_sums = lax.optimization_barrier(jnp.sum(difference * difference, axis=(1, 2)))
    penalty = lax.optimization_barrier(jnp.sum(feature_sums * norm_gain * norm_gain, axis=-1)) / (sigma_noise * sigma_noise * TOKENS * D)
    gain_grad = norm_gain * lax.optimization_barrier(jnp.sum(feature_sums, axis=0)) / (sigma_noise * sigma_noise * TOKENS)
    return (features, penalty, gain_grad)
```

```python
import functools
import math

import jax
import jax.numpy as jnp
from jax import lax
from jax.experimental import pallas as pl
from jax.experimental.pallas import tpu as pltpu
from jax.sharding import PartitionSpec as P

MESH = pl.DeviceIdType.MESH
HEAD_DIM = 128
SIGMA = 0.25
EPSILON = 1e-06
NEAR, FAR = 0, 1
BF = jnp.bfloat16
F32 = jnp.float32


def kernel(
    frames,
    clean_ref,
    noise_ref,
    weight_ref,
    gain_ref,
    counts_ref,
    features_ref,
    penalty_ref,
    grad_ref,
    streams,
    halo,
    gathered,
    staged,
    weights,
    total,
    squares,
    inverse,
    rows,
    pair,
    plane,
    points,
    line,
    halo_send,
    halo_recv,
    stage_sem,
    cross_sem,
    ring_send,
    ring_recv,
    relay_send,
    relay_recv,
    x_send,
    x_recv,
    row_send,
    row_recv,
    pair_sem,
    plane_send,
    plane_recv,
    point_send,
    point_recv,
    line_send,
    line_recv,
):
    depth = frames // 4
    tile = clean_ref.shape[2]
    width = clean_ref.shape[3]
    heads = width // HEAD_DIM
    f = lax.axis_index("frames")
    m = lax.axis_index("mp")
    lo = lax.axis_index("dp")
    core = f % 2
    hi = (f // 2) % 2
    z = f // 4
    up = 1 - 2 * core

    def at(z_, hi_, core_, m_, lo_):
        return (z_ * 4 + hi_ * 2 + core_, m_, lo_)

    sibling = at(z, hi, 1 - core, m, lo)
    far = ((f + frames + 2 * core - 1) % frames, m, lo)
    cross = at(z, 1 - hi, core, m, 1 - lo)
    onward = at((z + depth + up) % depth, hi, core, m, lo)

    def send(src, dst, send_sem, recv_sem, device):
        return pltpu.make_async_remote_copy(
            src_ref=src,
            dst_ref=dst,
            send_sem=send_sem,
            recv_sem=recv_sem,
            device_id=device,
            device_id_type=MESH,
        )

    y_peers = [at(z, (hi + a) % 2, core, m, (lo + b) % 2) for a, b in ((0, 1), (1, 0), (1, 1))]
    x_peers = [at(z, hi, core, (m + d) % 4, lo) for d in (1, 2, 3)]
    x_sources = [(m + 4 - d) % 4 for d in (1, 2, 3)]
    plane_peers = [at(z, (hi + a) % 2, core, (m + d) % 4, lo) for a in (0, 1) for d in (1, 2, 3)]
    z_peers = [at((z + d) % depth, hi, core, m, lo) for d in range(1, depth)]

    barrier = pltpu.get_barrier_semaphore()
    partners = [sibling, far] + y_peers + plane_peers + z_peers
    for device in partners:
        pl.semaphore_signal(barrier, inc=1, device_id=device, device_id_type=MESH)

    staged[core] = weight_ref[...].astype(F32)
    streams[0] = clean_ref[...]
    pl.semaphore_wait(barrier, len(partners))

    stage_copy = send(staged.at[core], staged.at[core], stage_sem.at[0], stage_sem.at[1], sibling)
    stage_copy.start()

    near_slot = 1 - core
    far_slot = core
    halo_copies = {}

    def send_halo(stream):
        for kind, slot, device in ((NEAR, near_slot, sibling), (FAR, far_slot, far)):
            halo_copies[kind, stream] = send(
                streams.at[stream, slot, pl.ds(1, 2)],
                halo.at[kind, stream],
                halo_send.at[kind, stream],
                halo_recv.at[kind, stream],
                device,
            )
            halo_copies[kind, stream].start()

    send_halo(0)
    for slot in range(2):
        for part in range(3):
            streams[1, slot, part] = (
                clean_ref[slot, part].astype(F32) + SIGMA * noise_ref[slot, part].astype(F32)
            ).astype(BF)
    send_halo(1)

    band = 2 * weight_ref.shape[0]
    group = width // (2 * band)

    def block(zz, side):
        start = pl.multiple_of((zz % group) * (2 * band) + side * band, 16)
        return weights.at[zz // group, pl.ds(start, band)]

    sides = (hi, 1 - hi)
    ring = {}
    relays = {}
    last = depth // 2 - 1

    def start_ring(chunk, step):
        side = sides[chunk] if step < last else (hi + core) % 2
        here = block((z + depth - up * step) % depth, side)
        ring[chunk, step] = send(
            here, here, ring_send.at[chunk, step], ring_recv.at[chunk, step], onward
        )
        ring[chunk, step].start()

    def service(step):
        for chunk in range(2 if step < last else 1):
            ring[chunk, step].wait_recv()
            side = sides[chunk] if step < last else (hi + core) % 2
            here = block((z + 2 * depth - up * (step + 1)) % depth, side)
            if step + 1 < last:
                start_ring(chunk, step + 1)
            relays[chunk, step] = send(
                here, here, relay_send.at[chunk, step], relay_recv.at[chunk, step], sibling
            )
            relays[chunk, step].start()
        if step + 1 == last:
            start_ring(0, last)

    stage_copy.wait()
    own = block(z, hi)
    own[...] = staged[...].reshape(band, width).astype(BF)
    start_ring(0, 0)
    cross_copy = send(own, own, cross_sem.at[0], cross_sem.at[1], cross)
    cross_copy.start()

    def live_count(index):
        inside = (index >= 0) & (index < 2 * frames)
        safe = jnp.clip(index, 0, 2 * frames - 1)
        return jnp.where(inside, counts_ref[0, safe], 0)

    own_slots = (near_slot, far_slot)
    own_counts = (live_count(2 * f + near_slot), live_count(2 * f + far_slot))
    other_counts = (live_count(2 * f + 2 - 3 * core), live_count(2 * f - 1 + 3 * core))
    scale = math.log2(math.e) / math.sqrt(HEAD_DIM)
    nt = (((1,), (1,)), ((), ()))
    nn = (((1,), (0,)), ((), ()))
    key_index = lax.broadcasted_iota(jnp.int32, (tile, tile), 1)

    def attention(kind, stream):
        slot = own_slots[kind]
        halo_copies[kind, stream].wait_recv()
        live_own = key_index < own_counts[kind]
        live_other = key_index < other_counts[kind]
        for h in range(heads):
            lanes = slice(h * HEAD_DIM, (h + 1) * HEAD_DIM)
            query = streams[stream, slot, 0, :, lanes]
            s_own = lax.dot_general(
                query, streams[stream, slot, 1, :, lanes], nt, preferred_element_type=F32
            )
            s_other = lax.dot_general(
                query, halo[kind, stream, 0, :, lanes], nt, preferred_element_type=F32
            )
            s_own = jnp.where(live_own, s_own * scale, -1e30)
            s_other = jnp.where(live_other, s_other * scale, -1e30)
            largest = jnp.max(jnp.maximum(s_own, s_other), axis=1, keepdims=True)
            p_own = jnp.exp2(s_own - largest)
            p_other = jnp.exp2(s_other - largest)
            norm = 1.0 / jnp.sum(p_own + p_other, axis=1, keepdims=True)
            mixed = lax.dot_general(
                (p_own * norm).astype(BF),
                streams[stream, slot, 2, :, lanes],
                nn,
                preferred_element_type=F32,
            ) + lax.dot_general(
                (p_other * norm).astype(BF),
                halo[kind, stream, 1, :, lanes],
                nn,
                preferred_element_type=F32,
            )
            gathered[m, kind, stream, :, lanes] = mixed.astype(BF)

    x_copies = []

    def send_attended(kind):
        for d in range(3):
            copy = send(
                gathered.at[m, kind],
                gathered.at[m, kind],
                x_send.at[kind, d],
                x_recv.at[kind, d],
                x_peers[d],
            )
            copy.start()
            x_copies.append(copy)

    attention(NEAR, 0)
    attention(NEAR, 1)
    send_attended(NEAR)
    cross_copy.wait()
    start_ring(1, 0)
    service(0)
    service(1)
    service(2)
    attention(FAR, 0)
    service(3)
    attention(FAR, 1)
    send_attended(FAR)
    for step in range(4, last + 1):
        service(step)

    for copy in halo_copies.values():
        copy.wait_send()
    for copy in ring.values():
        copy.wait_send()
    for copy in relays.values():
        copy.wait()
    for copy in x_copies:
        copy.wait()

    total[...] = jnp.zeros_like(total)

    @pl.loop(0, 4)
    def _(k):
        total[...] += jnp.dot(
            gathered[k].reshape(4 * tile, width), weights[k], preferred_element_type=F32
        )

    for g in range(4):
        part = jnp.zeros((tile, HEAD_DIM), F32)
        for h in range(heads):
            value = total[g * tile : (g + 1) * tile, h * HEAD_DIM : (h + 1) * HEAD_DIM]
            part += value * value
        squares[g * tile : (g + 1) * tile] = part
    rows[m] = jnp.sum(squares[...].T, axis=0, keepdims=True)
    row_copies = [
        send(rows.at[m], rows.at[m], row_send.at[d], row_recv.at[d], x_peers[d]) for d in range(3)
    ]
    for copy in row_copies:
        copy.start()
    for copy in row_copies:
        copy.wait()
    square = rows[0] + rows[1] + rows[2] + rows[3]
    inverse_row = lax.rsqrt(square / (4 * width) + EPSILON)
    inverse[...] = jnp.broadcast_to(inverse_row, (HEAD_DIM, 4 * tile)).T

    token = lax.broadcasted_iota(jnp.int32, (tile, HEAD_DIM), 0)
    for h in range(heads):
        lanes = slice(h * HEAD_DIM, (h + 1) * HEAD_DIM)
        gain = gain_ref[:, lanes]
        sums = jnp.zeros((1, HEAD_DIM), F32)
        for kind in range(2):
            live = (token < own_counts[kind]).astype(F32)
            base = 2 * kind * tile
            first, second = slice(base, base + tile), slice(base + tile, base + 2 * tile)
            normed = total[first, lanes] * inverse[first]
            features_ref[own_slots[kind], :, lanes] = (normed * gain * live).astype(BF)
            difference = (total[second, lanes] * inverse[second] - normed) * live
            sums += jnp.sum(difference * difference, axis=0, keepdims=True)
        pair[core, :, lanes] = sums

    pair_copy = send(pair.at[core], pair.at[core], pair_sem.at[0], pair_sem.at[1], sibling)
    pair_copy.start()
    pair_copy.wait()
    gain = gain_ref[...]
    pair_sum = pair[0] + pair[1]
    point = jnp.broadcast_to(
        jnp.sum(gain * gain * pair_sum, axis=1, keepdims=True), (1, HEAD_DIM)
    )
    y = hi * 2 + lo
    spot = m * 2 + hi
    plane[y] = jnp.concatenate([pair_sum, point], axis=1)
    points[spot] = point
    copies = [
        send(plane.at[y], plane.at[y], plane_send.at[i], plane_recv.at[i], y_peers[i])
        for i in range(3)
    ] + [
        send(points.at[spot], points.at[spot], point_send.at[i], point_recv.at[i], plane_peers[i])
        for i in range(6)
    ]
    for copy in copies:
        copy.start()
    for copy in copies:
        copy.wait()
    points[m * 2 + 1 - hi] = plane[(1 - hi) * 2 + lo, :, width:]
    point = points[0]
    for i in range(1, 8):
        point = point + points[i]
    plane_sum = plane[0] + plane[1] + plane[2] + plane[3]
    line[z] = jnp.concatenate([plane_sum[:, :width], point], axis=1)
    copies = [
        send(line.at[z], line.at[z], line_send.at[i], line_recv.at[i], z_peers[i])
        for i in range(depth - 1)
    ]
    for copy in copies:
        copy.start()
    for copy in copies:
        copy.wait()
    line_sum = line[0]
    for i in range(1, depth):
        line_sum = line_sum + line[i]
    tokens = 2.0 * frames * tile
    grad_ref[...] = gain * line_sum[:, :width] * (1.0 / (SIGMA * SIGMA * tokens))
    penalty_ref[...] = line_sum[:, width:] * (1.0 / (SIGMA * SIGMA * tokens * 4 * width))


def local(projections, perturbation, out_weight, norm_gain, live_counts):
    frames = lax.axis_size("frames")
    depth = frames // 4
    _, slots, tile, _, width = projections.shape
    clean = jnp.transpose(projections[0], (0, 2, 1, 3))
    noise = jnp.transpose(perturbation[0], (0, 2, 1, 3))
    steps = depth // 2
    dma = pltpu.SemaphoreType.DMA
    vmem = pl.BlockSpec(memory_space=pltpu.VMEM)
    features, penalty, grad = pl.pallas_call(
        functools.partial(kernel, frames),
        out_shape=(
            jax.ShapeDtypeStruct((slots, tile, width), BF),
            jax.ShapeDtypeStruct((1, HEAD_DIM), F32),
            jax.ShapeDtypeStruct((1, width), F32),
        ),
        in_specs=[vmem, vmem, vmem, vmem, pl.BlockSpec(memory_space=pltpu.SMEM)],
        out_specs=(vmem, vmem, vmem),
        scratch_shapes=[
            pltpu.VMEM((2, 2, 3, tile, width), BF),
            pltpu.VMEM((2, 2, 2, tile, width), BF),
            pltpu.VMEM((4, 2, 2, tile, width), BF),
            pltpu.VMEM((2, out_weight.shape[0], width), F32),
            pltpu.VMEM((4, width, width), BF),
            pltpu.VMEM((4 * tile, width), F32),
            pltpu.VMEM((4 * tile, HEAD_DIM), F32),
            pltpu.VMEM((4 * tile, HEAD_DIM), F32),
            pltpu.VMEM((4, 1, 4 * tile), F32),
            pltpu.VMEM((2, 1, width), F32),
            pltpu.VMEM((4, 1, width + HEAD_DIM), F32),
            pltpu.VMEM((8, 1, HEAD_DIM), F32),
            pltpu.VMEM((depth, 1, width + HEAD_DIM), F32),
            dma((2, 2)),
            dma((2, 2)),
            dma((2,)),
            dma((2,)),
            dma((2, steps)),
            dma((2, steps)),
            dma((2, steps)),
            dma((2, steps)),
            dma((2, 3)),
            dma((2, 3)),
            dma((3,)),
            dma((3,)),
            dma((2,)),
            dma((3,)),
            dma((3,)),
            dma((6,)),
            dma((6,)),
            dma((depth - 1,)),
            dma((depth - 1,)),
        ],
        compiler_params=pltpu.CompilerParams(
            collective_id=0, has_side_effects=True, vmem_limit_bytes=48 * 1024 * 1024
        ),
        name="attend_project_reduce",
    )(clean, noise, out_weight, norm_gain.reshape(1, width), live_counts)
    return features[None], penalty[0, :1], grad[0]


def solution(mesh):
    placed = (
        P("dp", "frames", None, None, "mp"),
        P("dp", "frames", None, None, "mp"),
        P("frames", "mp"),
        P("mp"),
        P("dp", None),
    )
    return jax.shard_map(
        local,
        mesh=mesh,
        in_specs=placed,
        out_specs=(P("dp", "frames", None, "mp"), P("dp"), P("mp")),
        check_vma=False,
    )
```

```python
import functools
import math

import jax
import jax.numpy as jnp
from jax import lax
from jax.experimental import pallas as pl
from jax.experimental.pallas import tpu as pltpu
from jax.sharding import PartitionSpec as P

MESH = pl.DeviceIdType.MESH
HEAD_DIM = 128
SIGMA = 0.25
EPSILON = 1e-06
NEAR, FAR = 0, 1
BF = jnp.bfloat16
F32 = jnp.float32


def kernel(
    frames,
    clean_ref,
    noise_ref,
    weight_ref,
    gain_ref,
    counts_ref,
    features_ref,
    penalty_ref,
    grad_ref,
    streams,
    noise,
    halo,
    gathered,
    raw,
    weights,
    total,
    squares,
    inverse,
    rows,
    gains,
    counts,
    pair,
    plane,
    points,
    line,
    load_sem,
    halo_send,
    halo_recv,
    raw_send,
    raw_recv,
    ring_send,
    ring_recv,
    relay_send,
    relay_recv,
    x_send,
    x_recv,
    row_send,
    row_recv,
    pair_sem,
    plane_send,
    plane_recv,
    point_send,
    point_recv,
    line_send,
    line_recv,
):
    depth = frames // 4
    tile = clean_ref.shape[2]
    width = clean_ref.shape[3]
    heads = width // HEAD_DIM
    f = lax.axis_index("frames")
    m = lax.axis_index("mp")
    lo = lax.axis_index("dp")
    core = f % 2
    hi = (f // 2) % 2
    z = f // 4
    up = 1 - 2 * core

    def at(z_, hi_, core_, m_, lo_):
        return (z_ * 4 + hi_ * 2 + core_, m_, lo_)

    sibling = at(z, hi, 1 - core, m, lo)
    far = ((f + frames + 2 * core - 1) % frames, m, lo)
    cross = at(z, 1 - hi, core, m, 1 - lo)
    onward = at((z + depth + up) % depth, hi, core, m, lo)

    def send(src, dst, send_sem, recv_sem, device):
        return pltpu.make_async_remote_copy(
            src_ref=src,
            dst_ref=dst,
            send_sem=send_sem,
            recv_sem=recv_sem,
            device_id=device,
            device_id_type=MESH,
        )

    y_peers = [at(z, (hi + a) % 2, core, m, (lo + b) % 2) for a, b in ((0, 1), (1, 0), (1, 1))]
    x_peers = [at(z, hi, core, (m + d) % 4, lo) for d in (1, 2, 3)]
    plane_peers = [at(z, (hi + a) % 2, core, (m + d) % 4, lo) for a in (0, 1) for d in (1, 2, 3)]
    z_peers = [at((z + d) % depth, hi, core, m, lo) for d in range(1, depth)]

    loads = [
        pltpu.make_async_copy(src, dst, load_sem.at[i])
        for i, (src, dst) in enumerate(
            (
                (weight_ref, raw.at[0, core]),
                (clean_ref, streams.at[0]),
                (noise_ref, noise),
                (gain_ref, gains.at[pl.ds(0, heads)]),
                (counts_ref, counts),
            )
        )
    ]
    for load in loads:
        load.start()

    barrier = pltpu.get_barrier_semaphore()
    partners = [sibling, far] + y_peers + plane_peers + z_peers
    for device in partners:
        pl.semaphore_signal(barrier, inc=1, device_id=device, device_id_type=MESH)
    loads[0].wait()
    loads[1].wait()
    pl.semaphore_wait(barrier, len(partners))

    mine = raw.at[0, core]
    theirs = raw.at[1, core]
    raw_copies = [
        send(mine, theirs, raw_send.at[0], raw_recv.at[0], cross),
        send(mine, mine, raw_send.at[1], raw_recv.at[1], sibling),
        send(theirs, theirs, raw_send.at[2], raw_recv.at[2], sibling),
    ]
    raw_copies[0].start()
    raw_copies[1].start()

    near_slot = 1 - core
    far_slot = core
    own_slots = (near_slot, far_slot)
    halo_copies = {}

    def send_halo(kind, stream):
        halo_copies[kind, stream] = send(
            streams.at[stream, own_slots[kind], pl.ds(1, 2)],
            halo.at[kind, stream],
            halo_send.at[kind, stream],
            halo_recv.at[kind, stream],
            (sibling, far)[kind],
        )
        halo_copies[kind, stream].start()

    send_halo(NEAR, 0)
    loads[2].wait()
    for kind in (NEAR, FAR):
        slot = own_slots[kind]
        for part in range(3):
            streams[1, slot, part] = (
                streams[0, slot, part].astype(F32) + SIGMA * noise[slot, part].astype(F32)
            ).astype(BF)
        if kind == NEAR:
            send_halo(NEAR, 1)

    band = 2 * weight_ref.shape[0]
    group = width // (2 * band)
    cuts = ((0, 64), (64, band - 64))

    def block(zz, side, cut):
        start = pl.multiple_of((zz % group) * (2 * band) + side * band + cut[0], 16)
        return weights.at[zz // group, pl.ds(start, cut[1])]

    sides = (hi, 1 - hi)
    last = depth // 2 - 1
    ring = {}
    relays = {}

    def pass_on(side, step, c):
        here = block((z + depth - up * step) % depth, sides[side], cuts[c])
        return send(
            here, here, ring_send.at[side, step, c], ring_recv.at[side, step, c], onward
        )

    def start_ring(side, step):
        for c in range(2):
            ring[side, step, c] = pass_on(side, step, c)
            ring[side, step, c].start()

    def assemble(side):
        joined = jnp.concatenate([raw[side, 0].astype(F32), raw[side, 1].astype(F32)], axis=0)
        block(z, sides[side], (0, band))[...] = joined.astype(BF)
        start_ring(side, 0)

    def final_copies(side):
        return [pass_on(side, last, c) for c in range(2)]

    def relay(side, step):
        for c in range(2):
            here = block((z + 2 * depth - up * (step + 1)) % depth, sides[side], cuts[c])
            yield c, send(
                here, here, relay_send.at[side, step, c], relay_recv.at[side, step, c], sibling
            )

    def service(side, step):
        copies = dict(relay(side, step))
        for c in range(2):
            ring[side, step, c].wait_recv()
            if step + 1 < last:
                ring[side, step + 1, c] = pass_on(side, step + 1, c)
                ring[side, step + 1, c].start()
            else:
                @pl.when(core == side)
                def _():
                    pass_on(side, last, c).start()

            relays[side, step, c] = copies[c]
            relays[side, step, c].start()

    def service_last(side):
        @pl.when(core == side)
        def _():
            copies = dict(relay(side, last))
            for c in range(2):
                pass_on(side, last, c).wait_recv()
                copies[c].start()

    def live_count(index):
        inside = (index >= 0) & (index < 2 * frames)
        safe = jnp.clip(index, 0, 2 * frames - 1)
        return jnp.where(inside, counts[0, safe], 0)

    loads[3].wait()
    loads[4].wait()
    own_counts = (live_count(2 * f + near_slot), live_count(2 * f + far_slot))
    other_counts = (live_count(2 * f + 2 - 3 * core), live_count(2 * f - 1 + 3 * core))
    scale = math.log2(math.e) / math.sqrt(HEAD_DIM)
    nt = (((1,), (1,)), ((), ()))
    nn = (((1,), (0,)), ((), ()))
    key_index = lax.broadcasted_iota(jnp.int32, (tile, tile), 1)
    x_copies = []

    def attention(kind, stream):
        slot = own_slots[kind]
        halo_copies[kind, stream].wait_recv()
        live_own = key_index < own_counts[kind]
        live_other = key_index < other_counts[kind]
        for h in range(heads):
            lanes = slice(h * HEAD_DIM, (h + 1) * HEAD_DIM)
            query = streams[stream, slot, 0, :, lanes]
            s_own = lax.dot_general(
                query, streams[stream, slot, 1, :, lanes], nt, preferred_element_type=F32
            )
            s_other = lax.dot_general(
                query, halo[kind, stream, 0, :, lanes], nt, preferred_element_type=F32
            )
            s_own = jnp.where(live_own, s_own * scale, -1e30)
            s_other = jnp.where(live_other, s_other * scale, -1e30)
            largest = jnp.max(jnp.maximum(s_own, s_other), axis=1, keepdims=True)
            p_own = jnp.exp2(s_own - largest)
            p_other = jnp.exp2(s_other - largest)
            norm = 1.0 / jnp.sum(p_own + p_other, axis=1, keepdims=True)
            mixed = lax.dot_general(
                (p_own * norm).astype(BF),
                streams[stream, slot, 2, :, lanes],
                nn,
                preferred_element_type=F32,
            ) + lax.dot_general(
                (p_other * norm).astype(BF),
                halo[kind, stream, 1, :, lanes],
                nn,
                preferred_element_type=F32,
            )
            gathered[m, kind, stream, :, lanes] = mixed.astype(BF)
        piece = gathered.at[m, kind, stream]
        for d in (1, 0, 2):
            copy = send(
                piece, piece, x_send.at[kind, stream, d], x_recv.at[kind, stream, d], x_peers[d]
            )
            copy.start()
            x_copies.append(copy)

    def wait_relays(side, step):
        for c in range(2):
            relays[side, step, c].wait()

    def multiply(part):
        k = part % 4
        total[...] += jnp.dot(
            gathered[k].reshape(4 * tile, width), weights[k], preferred_element_type=F32
        )

    raw_copies[1].wait()
    assemble(0)
    attention(NEAR, 0)
    raw_copies[0].wait_recv()
    raw_copies[2].start()
    raw_copies[2].wait()
    assemble(1)
    send_halo(FAR, 0)
    send_halo(FAR, 1)
    attention(NEAR, 1)
    service(0, 0)
    service(1, 0)
    service(0, 1)
    service(1, 1)
    service(0, 2)
    attention(FAR, 0)
    service(1, 2)
    service(0, 3)
    service(1, 3)
    service(0, 4)
    attention(FAR, 1)
    total[...] = jnp.zeros_like(total)
    service(1, 4)
    service(0, 5)
    service(1, 5)
    service(0, 6)
    for copy in x_copies:
        copy.wait()
    for step in range(5):
        for side in range(2):
            wait_relays(side, step)
    own_part = z // group
    nearer = jnp.where(z % group >= group // 2, 1, 3)
    multiply(own_part)
    multiply(own_part + nearer)
    service_last(0)
    service(1, 6)
    for step in range(5, last):
        for side in range(2):
            wait_relays(side, step)
    multiply(own_part + 4 - nearer)
    service_last(1)

    gains[heads:] = jnp.zeros((8 - heads, HEAD_DIM), F32)
    raw_copies[0].wait_send()
    for copy in halo_copies.values():
        copy.wait_send()
    for copy in ring.values():
        copy.wait_send()
    for side in range(2):
        copies = dict(relay(side, last))

        @pl.when(core == side)
        def _():
            for c in range(2):
                pass_on(side, last, c).wait_send()
                copies[c].wait_send()

        @pl.when(core != side)
        def _():
            for c in range(2):
                copies[c].wait_recv()

    multiply(own_part + 2)

    for g in range(4):
        part = jnp.zeros((tile, HEAD_DIM), F32)
        for h in range(heads):
            value = total[g * tile : (g + 1) * tile, h * HEAD_DIM : (h + 1) * HEAD_DIM]
            part += value * value
        squares[g * tile : (g + 1) * tile] = part
    rows[m] = jnp.sum(squares[...].T, axis=0, keepdims=True)
    row_copies = [
        send(rows.at[m], rows.at[m], row_send.at[d], row_recv.at[d], x_peers[d]) for d in (1, 0, 2)
    ]
    for copy in row_copies:
        copy.start()
    for copy in row_copies:
        copy.wait()
    square = rows[0] + rows[1] + rows[2] + rows[3]
    inverse_row = lax.rsqrt(square / (4 * width) + EPSILON)
    inverse[...] = jnp.broadcast_to(inverse_row, (HEAD_DIM, 4 * tile)).T

    token = lax.broadcasted_iota(jnp.int32, (tile, HEAD_DIM), 0)
    for h in range(heads):
        lanes = slice(h * HEAD_DIM, (h + 1) * HEAD_DIM)
        sums = jnp.zeros((1, HEAD_DIM), F32)
        for kind in range(2):
            live = (token < own_counts[kind]).astype(F32)
            base = 2 * kind * tile
            first, second = slice(base, base + tile), slice(base + tile, base + 2 * tile)
            normed = total[first, lanes] * inverse[first]
            features_ref[own_slots[kind], :, lanes] = (normed * gains[h : h + 1] * live).astype(BF)
            difference = (total[second, lanes] * inverse[second] - normed) * live
            sums += jnp.sum(difference * difference, axis=0, keepdims=True)
        pair[core, h : h + 1] = sums
    pair[core, heads:] = jnp.zeros((8 - heads, HEAD_DIM), F32)

    pair_copy = send(pair.at[core], pair.at[core], pair_sem.at[0], pair_sem.at[1], sibling)
    pair_copy.start()
    pair_copy.wait()
    gain = gains[...]
    is_sum = lax.broadcasted_iota(jnp.int32, (8, HEAD_DIM), 0) < heads
    pair_sum = pair[0] + pair[1]
    point = jnp.sum(
        jnp.sum(gain * gain * pair_sum, axis=0, keepdims=True), axis=1, keepdims=True
    )
    point = jnp.broadcast_to(point, (1, HEAD_DIM))
    y = hi * 2 + lo
    spot = m * 2 + hi
    plane[y] = jnp.where(is_sum, pair_sum, point)
    points[spot] = point
    copies = [
        send(plane.at[y], plane.at[y], plane_send.at[i], plane_recv.at[i], y_peers[i])
        for i in range(3)
    ] + [
        send(points.at[spot], points.at[spot], point_send.at[i], point_recv.at[i], plane_peers[i])
        for i in range(6)
    ]
    for copy in copies:
        copy.start()
    for copy in copies:
        copy.wait()
    points[m * 2 + 1 - hi] = plane[(1 - hi) * 2 + lo, heads : heads + 1]
    point = points[0]
    for i in range(1, 8):
        point = point + points[i]
    line[z] = jnp.where(is_sum, plane[0] + plane[1] + plane[2] + plane[3], point)
    copies = [
        send(line.at[z], line.at[z], line_send.at[i], line_recv.at[i], z_peers[i])
        for i in sorted(range(depth - 1), key=lambda i: -min(i + 1, depth - 1 - i))
    ]
    for copy in copies:
        copy.start()
    for copy in copies:
        copy.wait()
    line_sum = line[0]
    for i in range(1, depth):
        line_sum = line_sum + line[i]
    tokens = 2.0 * frames * tile
    grad_ref[...] = (gain * line_sum * (1.0 / (SIGMA * SIGMA * tokens)))[:heads]
    penalty_ref[...] = line_sum[heads:] * (1.0 / (SIGMA * SIGMA * tokens * 4 * width))


def local(projections, perturbation, out_weight, norm_gain, live_counts):
    frames = lax.axis_size("frames")
    depth = frames // 4
    _, slots, tile, _, width = projections.shape
    heads = width // HEAD_DIM
    clean = jnp.transpose(projections[0], (0, 2, 1, 3))
    noise = jnp.transpose(perturbation[0], (0, 2, 1, 3))
    steps = depth // 2
    dma = pltpu.SemaphoreType.DMA
    vmem = pl.BlockSpec(memory_space=pltpu.VMEM)
    hbm = pl.BlockSpec(memory_space=pltpu.HBM)
    features, penalty, grad = pl.pallas_call(
        functools.partial(kernel, frames),
        out_shape=(
            jax.ShapeDtypeStruct((slots, tile, width), BF),
            jax.ShapeDtypeStruct((8 - heads, HEAD_DIM), F32),
            jax.ShapeDtypeStruct((heads, HEAD_DIM), F32),
        ),
        in_specs=[hbm, hbm, hbm, hbm, hbm],
        out_specs=(vmem, vmem, vmem),
        scratch_shapes=[
            pltpu.VMEM((2, slots, 3, tile, width), BF),
            pltpu.VMEM((slots, 3, tile, width), BF),
            pltpu.VMEM((2, 2, 2, tile, width), BF),
            pltpu.VMEM((4, 2, 2, tile, width), BF),
            pltpu.VMEM((2, 2, out_weight.shape[0], width), BF),
            pltpu.VMEM((4, width, width), BF),
            pltpu.VMEM((4 * tile, width), F32),
            pltpu.VMEM((4 * tile, HEAD_DIM), F32),
            pltpu.VMEM((4 * tile, HEAD_DIM), F32),
            pltpu.VMEM((4, 1, 4 * tile), F32),
            pltpu.VMEM((8, HEAD_DIM), F32),
            pltpu.SMEM(live_counts.shape, jnp.int32),
            pltpu.VMEM((2, 8, HEAD_DIM), F32),
            pltpu.VMEM((4, 8, HEAD_DIM), F32),
            pltpu.VMEM((8, 1, HEAD_DIM), F32),
            pltpu.VMEM((depth, 8, HEAD_DIM), F32),
            dma((5,)),
            dma((2, 2)),
            dma((2, 2)),
            dma((3,)),
            dma((3,)),
            dma((2, steps, 2)),
            dma((2, steps, 2)),
            dma((2, steps, 2)),
            dma((2, steps, 2)),
            dma((2, 2, 3)),
            dma((2, 2, 3)),
            dma((3,)),
            dma((3,)),
            dma((2,)),
            dma((3,)),
            dma((3,)),
            dma((6,)),
            dma((6,)),
            dma((depth - 1,)),
            dma((depth - 1,)),
        ],
        compiler_params=pltpu.CompilerParams(
            collective_id=0, has_side_effects=True, vmem_limit_bytes=54000 * 1024
        ),
        name="attend_project_reduce",
    )(clean, noise, out_weight, norm_gain.reshape(heads, HEAD_DIM), live_counts)
    return features[None], penalty[0, :1], grad.reshape(width)


def solution(mesh):
    placed = (
        P("dp", "frames", None, None, "mp"),
        P("dp", "frames", None, None, "mp"),
        P("frames", "mp"),
        P("mp"),
        P("dp", None),
    )
    return jax.shard_map(
        local,
        mesh=mesh,
        in_specs=placed,
        out_specs=(P("dp", "frames", None, "mp"), P("dp"), P("mp")),
        check_vma=False,
    )
```

```python
import functools
import math

import jax
import jax.numpy as jnp
from jax import lax
from jax.experimental import pallas as pl
from jax.experimental.pallas import tpu as pltpu
from jax.sharding import PartitionSpec as P

MESH = pl.DeviceIdType.MESH
HEAD_DIM = 128
SIGMA = 0.25
EPSILON = 1e-06
NEAR, FAR = 0, 1
BF = jnp.bfloat16
F32 = jnp.float32


def kernel(
    frames,
    clean_ref,
    noise_ref,
    weight_ref,
    gain_ref,
    counts_ref,
    features_ref,
    penalty_ref,
    grad_ref,
    streams,
    noise,
    halo,
    gathered,
    raw,
    weights,
    total,
    squares,
    inverse,
    rows,
    gains,
    counts,
    pair,
    plane,
    points,
    line,
    load_sem,
    halo_send,
    halo_recv,
    raw_send,
    raw_recv,
    ring_send,
    ring_recv,
    relay_send,
    relay_recv,
    x_send,
    x_recv,
    row_send,
    row_recv,
    pair_sem,
    plane_send,
    plane_recv,
    point_send,
    point_recv,
    line_send,
    line_recv,
):
    depth = frames // 4
    tile = clean_ref.shape[2]
    width = clean_ref.shape[3]
    heads = width // HEAD_DIM
    f = lax.axis_index("frames")
    m = lax.axis_index("mp")
    lo = lax.axis_index("dp")
    core = f % 2
    hi = (f // 2) % 2
    z = f // 4
    up = 1 - 2 * core

    def at(z_, hi_, core_, m_, lo_):
        return (z_ * 4 + hi_ * 2 + core_, m_, lo_)

    sibling = at(z, hi, 1 - core, m, lo)
    far = ((f + frames + 2 * core - 1) % frames, m, lo)
    cross = at(z, 1 - hi, core, m, 1 - lo)
    onward = at((z + depth + up) % depth, hi, core, m, lo)

    def send(src, dst, send_sem, recv_sem, device):
        return pltpu.make_async_remote_copy(
            src_ref=src,
            dst_ref=dst,
            send_sem=send_sem,
            recv_sem=recv_sem,
            device_id=device,
            device_id_type=MESH,
        )

    y_peers = [at(z, (hi + a) % 2, core, m, (lo + b) % 2) for a, b in ((0, 1), (1, 0), (1, 1))]
    x_peers = [at(z, hi, core, (m + d) % 4, lo) for d in (1, 2, 3)]
    plane_peers = [at(z, (hi + a) % 2, core, (m + d) % 4, lo) for a in (0, 1) for d in (1, 2, 3)]
    z_peers = [at((z + d) % depth, hi, core, m, lo) for d in range(1, depth)]

    loads = [
        pltpu.make_async_copy(src, dst, load_sem.at[i])
        for i, (src, dst) in enumerate(
            (
                (weight_ref, raw.at[0, core]),
                (clean_ref, streams.at[0]),
                (noise_ref, noise),
                (gain_ref, gains.at[pl.ds(0, heads)]),
                (counts_ref, counts),
            )
        )
    ]
    for load in loads:
        load.start()

    barrier = pltpu.get_barrier_semaphore()
    partners = [sibling, far] + y_peers + plane_peers + z_peers
    for device in partners:
        pl.semaphore_signal(barrier, inc=1, device_id=device, device_id_type=MESH)
    loads[0].wait()
    loads[1].wait()
    pl.semaphore_wait(barrier, len(partners))

    mine = raw.at[0, core]
    theirs = raw.at[1, core]
    raw_copies = [
        send(mine, theirs, raw_send.at[0], raw_recv.at[0], cross),
        send(mine, mine, raw_send.at[1], raw_recv.at[1], sibling),
        send(theirs, theirs, raw_send.at[2], raw_recv.at[2], sibling),
    ]
    raw_copies[0].start()
    raw_copies[1].start()

    near_slot = 1 - core
    far_slot = core
    own_slots = (near_slot, far_slot)
    halo_copies = {}

    def send_halo(kind, stream):
        halo_copies[kind, stream] = send(
            streams.at[stream, own_slots[kind], pl.ds(1, 2)],
            halo.at[kind, stream],
            halo_send.at[kind, stream],
            halo_recv.at[kind, stream],
            (sibling, far)[kind],
        )
        halo_copies[kind, stream].start()

    send_halo(NEAR, 0)
    loads[2].wait()
    for kind in (NEAR, FAR):
        slot = own_slots[kind]
        for part in range(3):
            streams[1, slot, part] = (
                streams[0, slot, part].astype(F32) + SIGMA * noise[slot, part].astype(F32)
            ).astype(BF)
        if kind == NEAR:
            send_halo(NEAR, 1)

    band = 2 * weight_ref.shape[0]
    group = width // (2 * band)
    cuts = ((0, 64), (64, band - 64))

    def block(zz, side, cut):
        start = pl.multiple_of((zz % group) * (2 * band) + side * band + cut[0], 16)
        return weights.at[zz // group, pl.ds(start, cut[1])]

    sides = (hi, 1 - hi)
    last = depth // 2 - 1
    ring = {}
    relays = {}

    def pass_on(side, step, c):
        here = block((z + depth - up * step) % depth, sides[side], cuts[c])
        return send(
            here, here, ring_send.at[side, step, c], ring_recv.at[side, step, c], onward
        )

    def start_ring(side, step):
        for c in range(2):
            ring[side, step, c] = pass_on(side, step, c)
            ring[side, step, c].start()

    def assemble(side):
        joined = jnp.concatenate([raw[side, 0].astype(F32), raw[side, 1].astype(F32)], axis=0)
        block(z, sides[side], (0, band))[...] = joined.astype(BF)
        start_ring(side, 0)

    def final_copies(side):
        return [pass_on(side, last, c) for c in range(2)]

    def relay(side, step):
        for c in range(2):
            here = block((z + 2 * depth - up * (step + 1)) % depth, sides[side], cuts[c])
            yield c, send(
                here, here, relay_send.at[side, step, c], relay_recv.at[side, step, c], sibling
            )

    def service(side, step):
        copies = dict(relay(side, step))
        for c in range(2):
            ring[side, step, c].wait_recv()
            if step + 1 < last:
                ring[side, step + 1, c] = pass_on(side, step + 1, c)
                ring[side, step + 1, c].start()
            if step + 1 == last:

                @pl.when(core == side)
                def _():
                    pass_on(side, last, c).start()

        for c in range(2):
            relays[side, step, c] = copies[c]
            relays[side, step, c].start()

    def service_last(side):
        @pl.when(core == side)
        def _():
            copies = dict(relay(side, last))
            for c in range(2):
                pass_on(side, last, c).wait_recv()
                copies[c].start()

    def live_count(index):
        inside = (index >= 0) & (index < 2 * frames)
        safe = jnp.clip(index, 0, 2 * frames - 1)
        return jnp.where(inside, counts[0, safe], 0)

    loads[3].wait()
    loads[4].wait()
    own_counts = (live_count(2 * f + near_slot), live_count(2 * f + far_slot))
    other_counts = (live_count(2 * f + 2 - 3 * core), live_count(2 * f - 1 + 3 * core))
    scale = math.log2(math.e) / math.sqrt(HEAD_DIM)
    nt = (((1,), (1,)), ((), ()))
    nn = (((1,), (0,)), ((), ()))
    key_index = lax.broadcasted_iota(jnp.int32, (tile, tile), 1)
    x_copies = []

    def attention(kind, stream):
        slot = own_slots[kind]
        halo_copies[kind, stream].wait_recv()
        live_own = key_index < own_counts[kind]
        live_other = key_index < other_counts[kind]
        for h in range(heads):
            lanes = slice(h * HEAD_DIM, (h + 1) * HEAD_DIM)
            query = streams[stream, slot, 0, :, lanes]
            s_own = lax.dot_general(
                query, streams[stream, slot, 1, :, lanes], nt, preferred_element_type=F32
            )
            s_other = lax.dot_general(
                query, halo[kind, stream, 0, :, lanes], nt, preferred_element_type=F32
            )
            s_own = jnp.where(live_own, s_own * scale, -1e30)
            s_other = jnp.where(live_other, s_other * scale, -1e30)
            largest = jnp.max(jnp.maximum(s_own, s_other), axis=1, keepdims=True)
            p_own = jnp.exp2(s_own - largest)
            p_other = jnp.exp2(s_other - largest)
            norm = 1.0 / jnp.sum(p_own + p_other, axis=1, keepdims=True)
            mixed = lax.dot_general(
                (p_own * norm).astype(BF),
                streams[stream, slot, 2, :, lanes],
                nn,
                preferred_element_type=F32,
            ) + lax.dot_general(
                (p_other * norm).astype(BF),
                halo[kind, stream, 1, :, lanes],
                nn,
                preferred_element_type=F32,
            )
            gathered[m, kind, stream, :, lanes] = mixed.astype(BF)
        piece = gathered.at[m, kind, stream]
        for d in (1, 0, 2):
            copy = send(
                piece, piece, x_send.at[kind, stream, d], x_recv.at[kind, stream, d], x_peers[d]
            )
            copy.start()
            x_copies.append(copy)

    def wait_relays(side, step):
        for c in range(2):
            relays[side, step, c].wait()

    def multiply(part):
        k = part % 4
        total[...] += jnp.dot(
            gathered[k].reshape(4 * tile, width), weights[k], preferred_element_type=F32
        )

    raw_copies[1].wait()
    assemble(0)
    attention(NEAR, 0)
    raw_copies[0].wait_recv()
    raw_copies[2].start()
    raw_copies[2].wait()
    assemble(1)
    send_halo(FAR, 0)
    send_halo(FAR, 1)
    attention(NEAR, 1)
    service(0, 0)
    service(1, 0)
    service(0, 1)
    service(1, 1)
    service(0, 2)
    attention(FAR, 0)
    service(1, 2)
    service(0, 3)
    service(1, 3)
    service(0, 4)
    attention(FAR, 1)
    total[...] = jnp.zeros_like(total)
    service(1, 4)
    service(0, 5)
    service(1, 5)
    service(0, 6)
    service_last(0)
    for copy in x_copies:
        copy.wait()
    for step in range(5):
        for side in range(2):
            wait_relays(side, step)
    own_part = z // group
    nearer = jnp.where(z % group >= group // 2, 1, 3)
    multiply(own_part)
    service(1, 6)
    service_last(1)
    multiply(own_part + nearer)
    for step in range(5, last):
        for side in range(2):
            wait_relays(side, step)
    multiply(own_part + 4 - nearer)

    gains[heads:] = jnp.zeros((8 - heads, HEAD_DIM), F32)
    raw_copies[0].wait_send()
    for copy in halo_copies.values():
        copy.wait_send()
    for copy in ring.values():
        copy.wait_send()
    for side in range(2):
        copies = dict(relay(side, last))

        @pl.when(core == side)
        def _():
            for c in range(2):
                pass_on(side, last, c).wait_send()
                copies[c].wait_send()

        @pl.when(core != side)
        def _():
            for c in range(2):
                copies[c].wait_recv()

    multiply(own_part + 2)

    for g in range(4):
        part = jnp.zeros((tile, HEAD_DIM), F32)
        for h in range(heads):
            value = total[g * tile : (g + 1) * tile, h * HEAD_DIM : (h + 1) * HEAD_DIM]
            part += value * value
        squares[g * tile : (g + 1) * tile] = part
    rows[m] = jnp.sum(squares[...].T, axis=0, keepdims=True)
    row_copies = [
        send(rows.at[m], rows.at[m], row_send.at[d], row_recv.at[d], x_peers[d]) for d in (1, 0, 2)
    ]
    for copy in row_copies:
        copy.start()
    for copy in row_copies:
        copy.wait()
    square = rows[0] + rows[1] + rows[2] + rows[3]
    inverse_row = lax.rsqrt(square / (4 * width) + EPSILON)
    inverse[...] = jnp.broadcast_to(inverse_row, (HEAD_DIM, 4 * tile)).T

    token = lax.broadcasted_iota(jnp.int32, (tile, HEAD_DIM), 0)
    for h in range(heads):
        lanes = slice(h * HEAD_DIM, (h + 1) * HEAD_DIM)
        sums = jnp.zeros((1, HEAD_DIM), F32)
        for kind in range(2):
            live = (token < own_counts[kind]).astype(F32)
            base = 2 * kind * tile
            first, second = slice(base, base + tile), slice(base + tile, base + 2 * tile)
            normed = total[first, lanes] * inverse[first]
            features_ref[own_slots[kind], :, lanes] = (normed * gains[h : h + 1] * live).astype(BF)
            difference = (total[second, lanes] * inverse[second] - normed) * live
            sums += jnp.sum(difference * difference, axis=0, keepdims=True)
        pair[core, h : h + 1] = sums
    pair[core, heads:] = jnp.zeros((8 - heads, HEAD_DIM), F32)

    pair_copy = send(pair.at[core], pair.at[core], pair_sem.at[0], pair_sem.at[1], sibling)
    pair_copy.start()
    pair_copy.wait()
    gain = gains[...]
    is_sum = lax.broadcasted_iota(jnp.int32, (8, HEAD_DIM), 0) < heads
    pair_sum = pair[0] + pair[1]
    point = jnp.sum(
        jnp.sum(gain * gain * pair_sum, axis=0, keepdims=True), axis=1, keepdims=True
    )
    point = jnp.broadcast_to(point, (1, HEAD_DIM))
    y = hi * 2 + lo
    spot = m * 2 + hi
    plane[y] = jnp.where(is_sum, pair_sum, point)
    points[spot] = point
    copies = [
        send(plane.at[y], plane.at[y], plane_send.at[i], plane_recv.at[i], y_peers[i])
        for i in range(3)
    ] + [
        send(points.at[spot], points.at[spot], point_send.at[i], point_recv.at[i], plane_peers[i])
        for i in range(6)
    ]
    for copy in copies:
        copy.start()
    for copy in copies:
        copy.wait()
    points[m * 2 + 1 - hi] = plane[(1 - hi) * 2 + lo, heads : heads + 1]
    point = points[0]
    for i in range(1, 8):
        point = point + points[i]
    line[z] = jnp.where(is_sum, plane[0] + plane[1] + plane[2] + plane[3], point)
    copies = [
        send(line.at[z], line.at[z], line_send.at[i], line_recv.at[i], z_peers[i])
        for i in sorted(range(depth - 1), key=lambda i: -min(i + 1, depth - 1 - i))
    ]
    for copy in copies:
        copy.start()
    for copy in copies:
        copy.wait()
    line_sum = line[0]
    for i in range(1, depth):
        line_sum = line_sum + line[i]
    tokens = 2.0 * frames * tile
    grad_ref[...] = (gain * line_sum * (1.0 / (SIGMA * SIGMA * tokens)))[:heads]
    penalty_ref[...] = line_sum[heads:] * (1.0 / (SIGMA * SIGMA * tokens * 4 * width))


def local(projections, perturbation, out_weight, norm_gain, live_counts):
    frames = lax.axis_size("frames")
    depth = frames // 4
    _, slots, tile, _, width = projections.shape
    heads = width // HEAD_DIM
    clean = jnp.transpose(projections[0], (0, 2, 1, 3))
    noise = jnp.transpose(perturbation[0], (0, 2, 1, 3))
    steps = depth // 2
    dma = pltpu.SemaphoreType.DMA
    vmem = pl.BlockSpec(memory_space=pltpu.VMEM)
    hbm = pl.BlockSpec(memory_space=pltpu.HBM)
    features, penalty, grad = pl.pallas_call(
        functools.partial(kernel, frames),
        out_shape=(
            pltpu.VMEM((slots, tile, width), BF),
            pltpu.VMEM((8 - heads, HEAD_DIM), F32),
            pltpu.VMEM((heads, HEAD_DIM), F32),
        ),
        in_specs=[hbm, hbm, hbm, hbm, hbm],
        out_specs=(vmem, vmem, vmem),
        scratch_shapes=[
            pltpu.VMEM((2, slots, 3, tile, width), BF),
            pltpu.VMEM((slots, 3, tile, width), BF),
            pltpu.VMEM((2, 2, 2, tile, width), BF),
            pltpu.VMEM((4, 2, 2, tile, width), BF),
            pltpu.VMEM((2, 2, out_weight.shape[0], width), BF),
            pltpu.VMEM((4, width, width), BF),
            pltpu.VMEM((4 * tile, width), F32),
            pltpu.VMEM((4 * tile, HEAD_DIM), F32),
            pltpu.VMEM((4 * tile, HEAD_DIM), F32),
            pltpu.VMEM((4, 1, 4 * tile), F32),
            pltpu.VMEM((8, HEAD_DIM), F32),
            pltpu.SMEM(live_counts.shape, jnp.int32),
            pltpu.VMEM((2, 8, HEAD_DIM), F32),
            pltpu.VMEM((4, 8, HEAD_DIM), F32),
            pltpu.VMEM((8, 1, HEAD_DIM), F32),
            pltpu.VMEM((depth, 8, HEAD_DIM), F32),
            dma((5,)),
            dma((2, 2)),
            dma((2, 2)),
            dma((3,)),
            dma((3,)),
            dma((2, steps, 2)),
            dma((2, steps, 2)),
            dma((2, steps, 2)),
            dma((2, steps, 2)),
            dma((2, 2, 3)),
            dma((2, 2, 3)),
            dma((3,)),
            dma((3,)),
            dma((2,)),
            dma((3,)),
            dma((3,)),
            dma((6,)),
            dma((6,)),
            dma((depth - 1,)),
            dma((depth - 1,)),
        ],
        compiler_params=pltpu.CompilerParams(
            collective_id=0, has_side_effects=True, vmem_limit_bytes=56000 * 1024
        ),
        name="attend_project_reduce",
    )(clean, noise, out_weight, norm_gain.reshape(heads, HEAD_DIM), live_counts)
    return features[None], penalty[0, :1], grad.reshape(width)


def solution(mesh):
    placed = (
        P("dp", "frames", None, None, "mp"),
        P("dp", "frames", None, None, "mp"),
        P("frames", "mp"),
        P("mp"),
        P("dp", None),
    )
    return jax.shard_map(
        local,
        mesh=mesh,
        in_specs=placed,
        out_specs=(P("dp", "frames", None, "mp"), P("dp"), P("mp")),
        check_vma=False,
    )
```

```python
import functools
import math

import jax
import jax.numpy as jnp
from jax import lax
from jax.experimental import pallas as pl
from jax.experimental.pallas import tpu as pltpu
from jax.sharding import PartitionSpec as P

MESH = pl.DeviceIdType.MESH
HEAD_DIM = 128
SIGMA = 0.25
EPSILON = 1e-06
NEAR, FAR = 0, 1
BF = jnp.bfloat16
F32 = jnp.float32


def kernel(
    frames,
    clean_ref,
    noise_ref,
    weight_ref,
    gain_ref,
    counts_ref,
    features_ref,
    penalty_ref,
    grad_ref,
    streams,
    noise,
    halo,
    gathered,
    raw,
    weights,
    total,
    squares,
    inverse,
    rows,
    gains,
    counts,
    pair,
    plane,
    points,
    line,
    load_sem,
    halo_send,
    halo_recv,
    raw_send,
    raw_recv,
    ring_send,
    ring_recv,
    relay_send,
    relay_recv,
    x_send,
    x_recv,
    row_send,
    row_recv,
    pair_sem,
    plane_send,
    plane_recv,
    point_send,
    point_recv,
    line_send,
    line_recv,
):
    depth = frames // 4
    tile = clean_ref.shape[2]
    width = clean_ref.shape[3]
    heads = width // HEAD_DIM
    f = lax.axis_index("frames")
    m = lax.axis_index("mp")
    lo = lax.axis_index("dp")
    core = f % 2
    hi = (f // 2) % 2
    z = f // 4
    up = 1 - 2 * core

    def at(z_, hi_, core_, m_, lo_):
        return (z_ * 4 + hi_ * 2 + core_, m_, lo_)

    sibling = at(z, hi, 1 - core, m, lo)
    far = ((f + frames + 2 * core - 1) % frames, m, lo)
    cross = at(z, 1 - hi, core, m, 1 - lo)
    onward = at((z + depth + up) % depth, hi, core, m, lo)

    def send(src, dst, send_sem, recv_sem, device):
        return pltpu.make_async_remote_copy(
            src_ref=src,
            dst_ref=dst,
            send_sem=send_sem,
            recv_sem=recv_sem,
            device_id=device,
            device_id_type=MESH,
        )

    y_peers = [at(z, (hi + a) % 2, core, m, (lo + b) % 2) for a, b in ((0, 1), (1, 0), (1, 1))]
    x_peers = [at(z, hi, core, (m + d) % 4, lo) for d in (1, 2, 3)]
    plane_peers = [at(z, (hi + a) % 2, core, (m + d) % 4, lo) for a in (0, 1) for d in (1, 2, 3)]
    z_peers = [at((z + d) % depth, hi, core, m, lo) for d in range(1, depth)]

    loads = [
        pltpu.make_async_copy(src, dst, load_sem.at[i])
        for i, (src, dst) in enumerate(
            (
                (weight_ref, raw.at[0, core]),
                (clean_ref, streams.at[0]),
                (noise_ref, noise),
                (gain_ref, gains.at[pl.ds(0, heads)]),
                (counts_ref, counts),
            )
        )
    ]
    for load in loads:
        load.start()

    barrier = pltpu.get_barrier_semaphore()
    partners = [sibling, far] + y_peers + plane_peers + z_peers
    for device in partners:
        pl.semaphore_signal(barrier, inc=1, device_id=device, device_id_type=MESH)
    loads[0].wait()
    loads[1].wait()
    pl.semaphore_wait(barrier, len(partners))

    mine = raw.at[0, core]
    theirs = raw.at[1, core]
    raw_copies = [
        send(mine, theirs, raw_send.at[0], raw_recv.at[0], cross),
        send(mine, mine, raw_send.at[1], raw_recv.at[1], sibling),
        send(theirs, theirs, raw_send.at[2], raw_recv.at[2], sibling),
    ]
    raw_copies[0].start()
    raw_copies[1].start()

    near_slot = 1 - core
    far_slot = core
    own_slots = (near_slot, far_slot)
    halo_copies = {}

    def send_halo(kind, stream):
        halo_copies[kind, stream] = send(
            streams.at[stream, own_slots[kind], pl.ds(1, 2)],
            halo.at[kind, stream],
            halo_send.at[kind, stream],
            halo_recv.at[kind, stream],
            (sibling, far)[kind],
        )
        halo_copies[kind, stream].start()

    send_halo(NEAR, 0)
    loads[2].wait()
    for kind in (NEAR, FAR):
        slot = own_slots[kind]
        for part in range(3):
            streams[1, slot, part] = (
                streams[0, slot, part].astype(F32) + SIGMA * noise[slot, part].astype(F32)
            ).astype(BF)
        if kind == NEAR:
            send_halo(NEAR, 1)

    band = 2 * weight_ref.shape[0]
    group = width // (2 * band)
    cuts = ((0, 64), (64, band - 64))

    def block(zz, side, cut):
        start = pl.multiple_of((zz % group) * (2 * band) + side * band + cut[0], 16)
        return weights.at[zz // group, pl.ds(start, cut[1])]

    sides = (hi, 1 - hi)
    last = depth // 2 - 1
    ring = {}
    relays = {}

    def pass_on(side, step, c):
        here = block((z + depth - up * step) % depth, sides[side], cuts[c])
        return send(
            here, here, ring_send.at[side, step, c], ring_recv.at[side, step, c], onward
        )

    def start_ring(side, step):
        for c in range(2):
            ring[side, step, c] = pass_on(side, step, c)
            ring[side, step, c].start()

    def assemble(side):
        joined = jnp.concatenate([raw[side, 0].astype(F32), raw[side, 1].astype(F32)], axis=0)
        block(z, sides[side], (0, band))[...] = joined.astype(BF)
        start_ring(side, 0)

    def final_copies(side):
        return [pass_on(side, last, c) for c in range(2)]

    def relay(side, step):
        for c in range(2):
            here = block((z + 2 * depth - up * (step + 1)) % depth, sides[side], cuts[c])
            yield c, send(
                here, here, relay_send.at[side, step, c], relay_recv.at[side, step, c], sibling
            )

    def service(side, step):
        copies = dict(relay(side, step))
        for c in range(2):
            ring[side, step, c].wait_recv()
            if step + 1 < last:
                ring[side, step + 1, c] = pass_on(side, step + 1, c)
                ring[side, step + 1, c].start()
            if step + 1 == last:

                @pl.when(core == side)
                def _():
                    pass_on(side, last, c).start()

        for c in range(2):
            relays[side, step, c] = copies[c]
            relays[side, step, c].start()

    def service_last(side):
        @pl.when(core == side)
        def _():
            copies = dict(relay(side, last))
            for c in range(2):
                pass_on(side, last, c).wait_recv()
                copies[c].start()

    def live_count(index):
        inside = (index >= 0) & (index < 2 * frames)
        safe = jnp.clip(index, 0, 2 * frames - 1)
        return jnp.where(inside, counts[0, safe], 0)

    loads[3].wait()
    loads[4].wait()
    own_counts = (live_count(2 * f + near_slot), live_count(2 * f + far_slot))
    other_counts = (live_count(2 * f + 2 - 3 * core), live_count(2 * f - 1 + 3 * core))
    scale = math.log2(math.e) / math.sqrt(HEAD_DIM)
    nt = (((1,), (1,)), ((), ()))
    nn = (((1,), (0,)), ((), ()))
    key_index = lax.broadcasted_iota(jnp.int32, (tile, tile), 1)
    x_copies = []

    def attention(kind, stream):
        slot = own_slots[kind]
        halo_copies[kind, stream].wait_recv()
        live_own = key_index < own_counts[kind]
        live_other = key_index < other_counts[kind]
        for h in range(heads):
            lanes = slice(h * HEAD_DIM, (h + 1) * HEAD_DIM)
            query = streams[stream, slot, 0, :, lanes]
            s_own = lax.dot_general(
                query, streams[stream, slot, 1, :, lanes], nt, preferred_element_type=F32
            )
            s_other = lax.dot_general(
                query, halo[kind, stream, 0, :, lanes], nt, preferred_element_type=F32
            )
            s_own = jnp.where(live_own, s_own * scale, -1e30)
            s_other = jnp.where(live_other, s_other * scale, -1e30)
            largest = jnp.max(jnp.maximum(s_own, s_other), axis=1, keepdims=True)
            p_own = jnp.exp2(s_own - largest)
            p_other = jnp.exp2(s_other - largest)
            norm = 1.0 / jnp.sum(p_own + p_other, axis=1, keepdims=True)
            mixed = lax.dot_general(
                (p_own * norm).astype(BF),
                streams[stream, slot, 2, :, lanes],
                nn,
                preferred_element_type=F32,
            ) + lax.dot_general(
                (p_other * norm).astype(BF),
                halo[kind, stream, 1, :, lanes],
                nn,
                preferred_element_type=F32,
            )
            gathered[m, kind, stream, :, lanes] = mixed.astype(BF)
        piece = gathered.at[m, kind, stream]
        for d in (1, 0, 2):
            copy = send(
                piece, piece, x_send.at[kind, stream, d], x_recv.at[kind, stream, d], x_peers[d]
            )
            copy.start()
            x_copies.append(copy)

    def wait_relays(side, step):
        for c in range(2):
            relays[side, step, c].wait()

    def multiply(part):
        k = part % 4
        total[...] += jnp.dot(
            gathered[k].reshape(4 * tile, width), weights[k], preferred_element_type=F32
        )

    raw_copies[1].wait()
    assemble(0)
    attention(NEAR, 0)
    raw_copies[0].wait_recv()
    raw_copies[2].start()
    send_halo(FAR, 0)
    send_halo(FAR, 1)
    attention(NEAR, 1)
    raw_copies[2].wait()
    assemble(1)
    service(0, 0)
    service(1, 0)
    service(0, 1)
    service(1, 1)
    service(0, 2)
    attention(FAR, 0)
    service(1, 2)
    service(0, 3)
    service(1, 3)
    service(0, 4)
    attention(FAR, 1)
    total[...] = jnp.zeros_like(total)
    service(1, 4)
    service(0, 5)
    service(1, 5)
    service(0, 6)
    service_last(0)
    for copy in x_copies:
        copy.wait()
    for step in range(5):
        for side in range(2):
            wait_relays(side, step)
    own_part = z // group
    nearer = jnp.where(z % group >= group // 2, 1, 3)
    multiply(own_part)
    service(1, 6)
    service_last(1)
    multiply(own_part + nearer)
    for step in range(5, last):
        for side in range(2):
            wait_relays(side, step)
    multiply(own_part + 4 - nearer)

    gains[heads:] = jnp.zeros((8 - heads, HEAD_DIM), F32)
    raw_copies[0].wait_send()
    for copy in halo_copies.values():
        copy.wait_send()
    for copy in ring.values():
        copy.wait_send()
    for side in range(2):
        copies = dict(relay(side, last))

        @pl.when(core == side)
        def _():
            for c in range(2):
                pass_on(side, last, c).wait_send()
                copies[c].wait_send()

        @pl.when(core != side)
        def _():
            for c in range(2):
                copies[c].wait_recv()

    multiply(own_part + 2)

    for g in range(4):
        part = jnp.zeros((tile, HEAD_DIM), F32)
        for h in range(heads):
            value = total[g * tile : (g + 1) * tile, h * HEAD_DIM : (h + 1) * HEAD_DIM]
            part += value * value
        squares[g * tile : (g + 1) * tile] = part
    rows[m] = jnp.sum(squares[...].T, axis=0, keepdims=True)
    row_copies = [
        send(rows.at[m], rows.at[m], row_send.at[d], row_recv.at[d], x_peers[d]) for d in (1, 0, 2)
    ]
    for copy in row_copies:
        copy.start()
    for copy in row_copies:
        copy.wait()
    square = rows[0] + rows[1] + rows[2] + rows[3]
    inverse_row = lax.rsqrt(square / (4 * width) + EPSILON)
    inverse[...] = jnp.broadcast_to(inverse_row, (HEAD_DIM, 4 * tile)).T

    token = lax.broadcasted_iota(jnp.int32, (tile, HEAD_DIM), 0)
    for h in range(heads):
        lanes = slice(h * HEAD_DIM, (h + 1) * HEAD_DIM)
        sums = jnp.zeros((1, HEAD_DIM), F32)
        for kind in range(2):
            live = (token < own_counts[kind]).astype(F32)
            base = 2 * kind * tile
            first, second = slice(base, base + tile), slice(base + tile, base + 2 * tile)
            normed = total[first, lanes] * inverse[first]
            features_ref[own_slots[kind], :, lanes] = (normed * gains[h : h + 1] * live).astype(BF)
            difference = (total[second, lanes] * inverse[second] - normed) * live
            sums += jnp.sum(difference * difference, axis=0, keepdims=True)
        pair[core, h : h + 1] = sums
    pair[core, heads:] = jnp.zeros((8 - heads, HEAD_DIM), F32)

    pair_copy = send(pair.at[core], pair.at[core], pair_sem.at[0], pair_sem.at[1], sibling)
    pair_copy.start()
    pair_copy.wait()
    gain = gains[...]
    is_sum = lax.broadcasted_iota(jnp.int32, (8, HEAD_DIM), 0) < heads
    pair_sum = pair[0] + pair[1]
    point = jnp.sum(
        jnp.sum(gain * gain * pair_sum, axis=0, keepdims=True), axis=1, keepdims=True
    )
    point = jnp.broadcast_to(point, (1, HEAD_DIM))
    y = hi * 2 + lo
    spot = m * 2 + hi
    plane[y] = jnp.where(is_sum, pair_sum, point)
    points[spot] = point
    copies = [
        send(plane.at[y], plane.at[y], plane_send.at[i], plane_recv.at[i], y_peers[i])
        for i in range(3)
    ] + [
        send(points.at[spot], points.at[spot], point_send.at[i], point_recv.at[i], plane_peers[i])
        for i in range(6)
    ]
    for copy in copies:
        copy.start()
    for copy in copies:
        copy.wait()
    points[m * 2 + 1 - hi] = plane[(1 - hi) * 2 + lo, heads : heads + 1]
    point = points[0]
    for i in range(1, 8):
        point = point + points[i]
    line[z] = jnp.where(is_sum, plane[0] + plane[1] + plane[2] + plane[3], point)
    copies = [
        send(line.at[z], line.at[z], line_send.at[i], line_recv.at[i], z_peers[i])
        for i in sorted(range(depth - 1), key=lambda i: -min(i + 1, depth - 1 - i))
    ]
    for copy in copies:
        copy.start()
    for copy in copies:
        copy.wait()
    line_sum = line[0]
    for i in range(1, depth):
        line_sum = line_sum + line[i]
    tokens = 2.0 * frames * tile
    grad_ref[...] = (gain * line_sum * (1.0 / (SIGMA * SIGMA * tokens)))[:heads]
    penalty_ref[...] = line_sum[heads:] * (1.0 / (SIGMA * SIGMA * tokens * 4 * width))


def local(projections, perturbation, out_weight, norm_gain, live_counts):
    frames = lax.axis_size("frames")
    depth = frames // 4
    _, slots, tile, _, width = projections.shape
    heads = width // HEAD_DIM
    clean = jnp.transpose(projections[0], (0, 2, 1, 3))
    noise = jnp.transpose(perturbation[0], (0, 2, 1, 3))
    steps = depth // 2
    dma = pltpu.SemaphoreType.DMA
    vmem = pl.BlockSpec(memory_space=pltpu.VMEM)
    hbm = pl.BlockSpec(memory_space=pltpu.HBM)
    features, penalty, grad = pl.pallas_call(
        functools.partial(kernel, frames),
        out_shape=(
            pltpu.VMEM((slots, tile, width), BF),
            pltpu.VMEM((8 - heads, HEAD_DIM), F32),
            pltpu.VMEM((heads, HEAD_DIM), F32),
        ),
        in_specs=[hbm, hbm, hbm, hbm, hbm],
        out_specs=(vmem, vmem, vmem),
        scratch_shapes=[
            pltpu.VMEM((2, slots, 3, tile, width), BF),
            pltpu.VMEM((slots, 3, tile, width), BF),
            pltpu.VMEM((2, 2, 2, tile, width), BF),
            pltpu.VMEM((4, 2, 2, tile, width), BF),
            pltpu.VMEM((2, 2, out_weight.shape[0], width), BF),
            pltpu.VMEM((4, width, width), BF),
            pltpu.VMEM((4 * tile, width), F32),
            pltpu.VMEM((4 * tile, HEAD_DIM), F32),
            pltpu.VMEM((4 * tile, HEAD_DIM), F32),
            pltpu.VMEM((4, 1, 4 * tile), F32),
            pltpu.VMEM((8, HEAD_DIM), F32),
            pltpu.SMEM(live_counts.shape, jnp.int32),
            pltpu.VMEM((2, 8, HEAD_DIM), F32),
            pltpu.VMEM((4, 8, HEAD_DIM), F32),
            pltpu.VMEM((8, 1, HEAD_DIM), F32),
            pltpu.VMEM((depth, 8, HEAD_DIM), F32),
            dma((5,)),
            dma((2, 2)),
            dma((2, 2)),
            dma((3,)),
            dma((3,)),
            dma((2, steps, 2)),
            dma((2, steps, 2)),
            dma((2, steps, 2)),
            dma((2, steps, 2)),
            dma((2, 2, 3)),
            dma((2, 2, 3)),
            dma((3,)),
            dma((3,)),
            dma((2,)),
            dma((3,)),
            dma((3,)),
            dma((6,)),
            dma((6,)),
            dma((depth - 1,)),
            dma((depth - 1,)),
        ],
        compiler_params=pltpu.CompilerParams(
            collective_id=0, has_side_effects=True, vmem_limit_bytes=56000 * 1024
        ),
        name="attend_project_reduce",
    )(clean, noise, out_weight, norm_gain.reshape(heads, HEAD_DIM), live_counts)
    return features[None], penalty[0, :1], grad.reshape(width)


def solution(mesh):
    placed = (
        P("dp", "frames", None, None, "mp"),
        P("dp", "frames", None, None, "mp"),
        P("frames", "mp"),
        P("mp"),
        P("dp", None),
    )
    return jax.shard_map(
        local,
        mesh=mesh,
        in_specs=placed,
        out_specs=(P("dp", "frames", None, "mp"), P("dp"), P("mp")),
        check_vma=False,
    )
```
